32 devices in a mesh: gx: 8 (over z, y), gy: 4 (over x, core).
Axes of the slice: x: 2, y: 2, z: 4, core: 2. Of those that a mesh axis runs over, the one named last changes fastest.
Arguments:
- features: bfloat16 [1024, 256, 128], P('gx', 'gy'), may hold values from -6 to 6
- cotangent: bfloat16 [1024, 256, 128], P('gx', 'gy'), may hold values from -31 to 31
- kernel: float32 [7, 7, 128], replicated, may hold values from -0.875 to 0.875
- kernel_bias: float32 [128], replicated, may hold values from -3 to 3
- norm_gain: float32 [128], replicated, may hold values from 0.1 to 1.9
- norm_shift: float32 [128], replicated, may hold values from -3 to 3
- w_up: bfloat16 [128, 512], replicated, may hold values from -0.5 to 0.5
- b_up: float32 [512], replicated, may hold values from -3 to 3
- w_down: bfloat16 [512, 128], replicated, may hold values from -0.25 to 0.25
- b_down: float32 [128], replicated, may hold values from -3 to 3
- layer_scale: float32 [128], replicated, may hold values from 0.3 to 3
Outputs:
- d_features: bfloat16 [1024, 256, 128], P('gx', 'gy')
- d_kernel: float32 [7, 7, 128], replicated
- d_kernel_bias: float32 [128], replicated
- d_norm_gain: float32 [128], replicated
- d_norm_shift: float32 [128], replicated
- d_w_up: float32 [128, 512], replicated
- d_b_up: float32 [512], replicated
- d_w_down: float32 [512, 128], replicated
- d_b_down: float32 [128], replicated
- d_layer_scale: float32 [128], replicated
The draws below stay inside these ranges and needn't reach their ends.
All inputs are finite; a program needn't handle non-finite values.
Results may differ from the reference program's by a relative error of at most 0.0072.
Values may be sent and summed in bfloat16 or wider, within the bound.
A program may use at most 64 MiB of HBM per device.

```python
import math
import jax
import jax.numpy as jnp
from jax import lax

C = 128
E = 512
TAPS = 7
NH = 1024
NW = 256


def draw_cotangent(key, part):
    key_base = jax.random.fold_in(key, 11)
    key_rough = jax.random.fold_in(key, 23)
    base_values = jnp.clip(jax.random.normal(key_base, (NH, NW, C), jnp.float32), -5.0, 5.0)
    rough_factor = jnp.exp(jax.random.uniform(key_rough, (NH, NW, 1), jnp.float32, -0.7, 0.7))
    ramp_factor = 1.0 + 2.0 * jnp.arange(NH, dtype=jnp.float32) / NH
    return (base_values * rough_factor * ramp_factor[:, None, None]).astype(jnp.bfloat16)


def level_of(rng, shape, pieces, smallest, high):
    gain, own = 1.0, jax.random.fold_in(rng, 6)
    for axis_at, blocks in pieces:
        draws = jnp.exp(jax.random.uniform(jax.random.fold_in(own, axis_at), (blocks,), jnp.float32, smallest / len(pieces), high / len(pieces)))
        gain = gain * jnp.repeat(draws, shape[axis_at] // blocks).reshape([-1 if axis == axis_at else 1 for axis in range(len(shape))])
    return gain


def scatter_about(key, dims, deviation, reach, cuts=(), kind=jnp.bfloat16):
    values = jax.random.normal(key, dims, jnp.float32) * deviation
    if len(cuts) > 0:
        values = level_of(key, dims, cuts, -0.22, 0.18) * values
    return jnp.clip(values, min=-reach, max=reach).astype(kind)


def setup_inputs(seed: int = 0) -> dict:
    seeds = jax.random.split(jax.random.key(seed), 12)
    features = scatter_about(seeds[0], (NH, NW, C), 1.0, 6.0, ((0, 8), (1, 4)))
    cotangent = draw_cotangent(jax.random.fold_in(seeds[11], 71), 0)
    kernel = scatter_about(seeds[2], (TAPS, TAPS, C), (TAPS * TAPS) ** -0.5, 0.875, (), jnp.float32)
    kernel_bias = scatter_about(seeds[3], (C,), 0.5, 3.0, (), jnp.float32)
    norm_gain = jnp.clip(1.0 + 0.18 * jax.random.normal(seeds[4], (C,), jnp.float32), 0.1, 1.9)
    norm_shift = scatter_about(seeds[5], (C,), 0.5, 3.0, (), jnp.float32)
    w_up = scatter_about(seeds[6], (C, E), C ** -0.5, 0.5)
    b_up = scatter_about(seeds[7], (E,), 0.5, 3.0, (), jnp.float32)
    w_down = scatter_about(seeds[8], (E, C), E ** -0.5, 0.25)
    b_down = scatter_about(seeds[9], (C,), 0.5, 3.0, (), jnp.float32)
    layer_scale = jnp.clip(jnp.exp(jax.random.uniform(seeds[10], (C,), jnp.float32, math.log(0.3), math.log(3.0))), 0.3, 3.0)
    return dict(features=features, cotangent=cotangent, kernel=kernel, kernel_bias=kernel_bias, norm_gain=norm_gain, norm_shift=norm_shift, w_up=w_up, b_up=b_up, w_down=w_down, b_down=b_down, layer_scale=layer_scale)


EPSILON = 1e-06

def gelu_pair(hidden):
    erf_part = jax.scipy.special.erf(hidden * 0.7071067811865476)
    value = 0.5 * hidden * (1.0 + erf_part)
    slope_value = 0.5 * (1.0 + erf_part) + hidden * jnp.exp(-0.5 * hidden * hidden) * 0.3989422804014327
    return (value, slope_value)

def product(spec, left, right):
    return jnp.einsum(spec, left.astype(jnp.float32), right.astype(jnp.float32))

def depthwise(padded, kernel, row_count, col_count):
    tap_count = kernel.shape[0]
    accum = jnp.zeros((row_count, col_count, kernel.shape[2]), jnp.float32)
    for row_tap in range(tap_count):
        for col_tap in range(tap_count):
            window = padded[row_tap:row_tap + row_count, col_tap:col_tap + col_count]
            accum = accum + window.astype(jnp.float32) * kernel[row_tap, col_tap]
    return accum

def spread_back(padded, kernel, row_count, col_count):
    tap_count = kernel.shape[0]
    edge_cells = tap_count - 1
    accum = jnp.zeros((row_count, col_count, kernel.shape[2]), jnp.float32)
    for row_tap in range(tap_count):
        for col_tap in range(tap_count):
            window = padded[edge_cells - row_tap:edge_cells - row_tap + row_count, edge_cells - col_tap:edge_cells - col_tap + col_count]
            accum = accum + window * kernel[row_tap, col_tap]
    return accum

def kernel_grad(slopes_in, padded, tap_count):
    row_count, col_count = (slopes_in.shape[0], slopes_in.shape[1])
    rows_out = []
    for row_tap in range(tap_count):
        line = []
        for col_tap in range(tap_count):
            window = padded[row_tap:row_tap + row_count, col_tap:col_tap + col_count].astype(jnp.float32)
            line.append(lax.optimization_barrier(jnp.sum(slopes_in * window, axis=(0, 1))))
        rows_out.append(jnp.stack(line, 0))
    return jnp.stack(rows_out, 0)

def layer_back(conv_out, cotan, norm_gain, norm_shift, w_up, b_up, w_down, b_down, layer_scale, row_lo, row_hi, col_lo, col_hi):
    chan_mean = lax.optimization_barrier(jnp.mean(conv_out, axis=-1, keepdims=True))
    centred = conv_out - chan_mean
    inv_std = lax.rsqrt(lax.optimization_barrier(jnp.mean(centred * centred, axis=-1, keepdims=True)) + EPSILON)
    normed = centred * inv_std
    normal_out = (normed * norm_gain + norm_shift).astype(jnp.bfloat16)
    hidden = product('rwc,ce->rwe', normal_out, w_up) + b_up
    active, gelu_slope = gelu_pair(hidden)
    active = active.astype(jnp.bfloat16)
    output = product('rwe,ec->rwc', active, w_down) + b_down
    cot_float = cotan.astype(jnp.float32)
    d_output = (cot_float * layer_scale).astype(jnp.bfloat16)
    d_active = product('rwc,ec->rwe', d_output, w_down)
    d_hidden = (d_active * gelu_slope).astype(jnp.bfloat16)
    d_normal = product('rwe,ce->rwc', d_hidden, w_up)
    d_normed = d_normal * norm_gain
    first_mean = lax.optimization_barrier(jnp.mean(d_normed, axis=-1, keepdims=True))
    second_mean = lax.optimization_barrier(jnp.mean(d_normed * normed, axis=-1, keepdims=True))
    d_conv = inv_std * (d_normed - first_mean - normed * second_mean)
    rsel = slice(row_lo, row_hi)
    csel = slice(col_lo, col_hi)
    d_gain = lax.optimization_barrier(jnp.sum((d_normal * normed)[rsel, csel], axis=(0, 1)))
    d_shift = lax.optimization_barrier(jnp.sum(d_normal[rsel, csel], axis=(0, 1)))
    d_wup = product('rwc,rwe->ce', normal_out[rsel, csel], d_hidden[rsel, csel])
    d_bup = lax.optimization_barrier(jnp.sum(d_hidden[rsel, csel].astype(jnp.float32), axis=(0, 1)))
    d_wdown = product('rwe,rwc->ec', active[rsel, csel], d_output[rsel, csel])
    d_bdown = lax.optimization_barrier(jnp.sum(d_output[rsel, csel].astype(jnp.float32), axis=(0, 1)))
    d_lscale = lax.optimization_barrier(jnp.sum((cot_float * output)[rsel, csel], axis=(0, 1)))
    return (d_conv, (d_gain, d_shift, d_wup, d_bup, d_wdown, d_bdown, d_lscale))

def reference(features, cotangent, kernel, kernel_bias, norm_gain, norm_shift, w_up, b_up, w_down, b_down, layer_scale):
    tap_count = kernel.shape[0]
    reach_cells = tap_count // 2
    deep = 2 * reach_cells
    wrapped_x = jnp.concatenate([features[NH - deep:], features, features[:deep]], axis=0)
    padded_x = jnp.pad(wrapped_x, ((0, 0), (deep, deep), (0, 0)))
    wrapped_c = jnp.concatenate([cotangent[NH - reach_cells:], cotangent, cotangent[:reach_cells]], axis=0)
    padded_c = jnp.pad(wrapped_c, ((0, 0), (reach_cells, reach_cells), (0, 0)))
    block_rows = math.gcd(NH, 128)
    block_count = NH // block_rows
    col_place = lax.iota(jnp.int32, NW + 2 * reach_cells) - reach_cells
    keep_mask = (col_place >= 0) & (col_place < NW)

    def step(running, block_index):
        row_start = (block_index * block_rows).astype(jnp.int32)
        zero_index = jnp.zeros((), jnp.int32)
        x_block = lax.dynamic_slice(padded_x, (row_start, zero_index, zero_index), (block_rows + 2 * deep, NW + 2 * deep, C))
        c_block = lax.dynamic_slice(padded_c, (row_start, zero_index, zero_index), (block_rows + deep, NW + deep, C))
        conv_out = depthwise(x_block, kernel, block_rows + deep, NW + deep) + kernel_bias
        d_conv, layer_grads = layer_back(conv_out, c_block, norm_gain, norm_shift, w_up, b_up, w_down, b_down, layer_scale, reach_cells, reach_cells + block_rows, reach_cells, reach_cells + NW)
        d_conv = jnp.where(keep_mask[None, :, None], d_conv, 0.0)
        inner_slope = d_conv[reach_cells:reach_cells + block_rows, reach_cells:reach_cells + NW]
        inner_x = x_block[reach_cells:reach_cells + block_rows + deep, reach_cells:reach_cells + NW + deep]
        d_kern = kernel_grad(inner_slope, inner_x, tap_count)
        d_kbias = lax.optimization_barrier(jnp.sum(inner_slope, axis=(0, 1)))
        spread = spread_back(d_conv, kernel, block_rows, NW)
        own_cot = c_block[reach_cells:reach_cells + block_rows, reach_cells:reach_cells + NW].astype(jnp.float32)
        d_block = (own_cot + spread).astype(jnp.bfloat16)
        fresh = (d_kern, d_kbias) + layer_grads
        updated = tuple((old + new for old, new in zip(running, fresh)))
        return (updated, d_block)
    initial = (jnp.zeros((tap_count, tap_count, C), jnp.float32), jnp.zeros((C,), jnp.float32), jnp.zeros((C,), jnp.float32), jnp.zeros((C,), jnp.float32), jnp.zeros((C, E), jnp.float32), jnp.zeros((E,), jnp.float32), jnp.zeros((E, C), jnp.float32), jnp.zeros((C,), jnp.float32), jnp.zeros((C,), jnp.float32))
    sums, blocks = lax.scan(step, initial, jnp.arange(block_count, dtype=jnp.int32))
    d_features = blocks.reshape(NH, NW, C)
    factor = 1.0 / math.sqrt(NH * NW)
    d_kern, d_kbias, d_gain, d_shift, d_wup, d_bup, d_wdown, d_bdown, d_lscale = sums
    return (d_features, d_kern * factor, d_kbias * factor, d_gain * factor, d_shift * factor, d_wup * factor, d_bup * factor, d_wdown * factor, d_bdown * factor, d_lscale * factor)
```

```python
import functools
import math

import jax
import jax.numpy as jnp
from jax import lax
from jax.experimental import pallas as pl
from jax.experimental.pallas import tpu as pltpu
from jax.sharding import PartitionSpec as P

EPSILON = 1e-06
F32 = jnp.float32
BF16 = jnp.bfloat16
VMEM_BYTES = 60 * 1024 * 1024


def dot(left, right):
    return jnp.dot(left, right, preferred_element_type=F32)


def extended(cells, sides, width):
    for axis, dim in sides:
        count = lax.axis_size(axis)
        head = lax.slice_in_dim(cells, 0, width, axis=dim)
        tail = lax.slice_in_dim(cells, cells.shape[dim] - width, cells.shape[dim], axis=dim)
        cells = jnp.concatenate(
            [
                lax.ppermute(tail, axis, [(i, (i + 1) % count) for i in range(count)]),
                cells,
                lax.ppermute(head, axis, [((i + 1) % count, i) for i in range(count)]),
            ],
            axis=dim,
        )
    return cells


def mask_edges(padded, width):
    col_total = padded.shape[1]
    inner_cols = col_total - 2 * width
    grid_cols = inner_cols * lax.axis_size("gy")
    col_place = lax.axis_index("gy") * inner_cols + lax.iota(jnp.int32, col_total) - width
    keep_mask = (col_place >= 0) & (col_place < grid_cols)
    return jnp.where(keep_mask[None, :, None], padded, jnp.zeros((), padded.dtype))


def widened(cells, reach):
    padded = mask_edges(extended(cells, (("gx", 0), ("gy", 1)), reach), reach)
    extra = -padded.shape[1] % 16
    return jnp.pad(padded, ((0, 0), (0, extra), (0, 0)))


def tap_weights(kernel):
    taps, _, chans = kernel.shape
    pairs = (taps + 1) // 2
    framed = jnp.pad(kernel, ((1, 1), (0, 0), (0, 0)))
    eye = jnp.eye(chans, dtype=F32)
    blocks = []
    for q in range(pairs):
        top = jnp.concatenate([framed[2 * q + 1, :, :, None] * eye, framed[2 * q, :, :, None] * eye], 2)
        low = jnp.concatenate([framed[2 * q + 2, :, :, None] * eye, framed[2 * q + 1, :, :, None] * eye], 2)
        blocks.append(jnp.concatenate([top, low], 1).reshape(taps * 2 * chans, 2 * chans))
    return jnp.stack(blocks).astype(BF16)


def spread_taps(padded, wide, shifted, taps):
    pairs, cols, _ = shifted.shape
    chans = padded.shape[2]

    def one(j, carry):
        for s in range(2):
            wide[s] = padded[2 * j + s].astype(F32)
            for b in range(taps):
                at = (2 * b + s) * chans
                shifted[j, :, at : at + chans] = wide[s, b : b + cols, :].astype(BF16)
        return carry

    lax.fori_loop(0, pairs, one, 0)


def conv_pairs(shifted, weights, first, count):
    pairs, cols, depth = shifted.shape
    total = None
    for q in range(weights.shape[0]):
        rows = shifted[pl.ds(first + q, count)].reshape(count * cols, depth)
        part = dot(rows, weights[q])
        total = part if total is None else total + part
    return total


def forward_back(
    taps,
    count,
    padded,
    cot,
    conv_w,
    kbias,
    gain,
    shift,
    w_up,
    w_up_t,
    b_up,
    w_dn_t,
    d_conv,
    g_up,
    g_dn,
    g_bup,
    g_small,
    g_kern,
    wide,
    shifted,
    d_turned,
):
    rows, cols, chans = cot.shape
    half = count * cols
    spread_taps(padded, wide, shifted, taps)
    g_up[...] = jnp.zeros_like(g_up)
    g_dn[...] = jnp.zeros_like(g_dn)
    g_bup[...] = jnp.zeros_like(g_bup)
    g_small[...] = jnp.zeros_like(g_small)

    def chunk(i, carry):
        first = i * count
        pair_out = conv_pairs(shifted, conv_w, first, count)
        conv = jnp.concatenate([pair_out[:, :chans], pair_out[:, chans:]], 0) + kbias[...]
        cot_rows = [cot[2 * (first + k) + p] for p in range(2) for k in range(count)]
        cotan = jnp.concatenate(cot_rows, 0)
        centred = conv - jnp.mean(conv, axis=-1, keepdims=True)
        inv_std = lax.rsqrt(jnp.mean(centred * centred, axis=-1, keepdims=True) + EPSILON)
        normed = centred * inv_std
        normal_out = (normed * gain[...] + shift[...]).astype(BF16)
        hidden = dot(normal_out, w_up[...]) + b_up[...]
        bell = jnp.exp(hidden * hidden * -0.5)
        place = 1.0 / (1.0 + jnp.abs(hidden) * (0.3275911 * 0.7071067811865476))
        tail = place * (
            0.127414796
            + place * (-0.142248368 + place * (0.7107068705 + place * (-0.7265760135 + place * 0.5307027145)))
        )
        tail = tail * bell
        phi = jnp.where(hidden >= 0.0, 1.0 - tail, tail)
        active = (hidden * phi).astype(BF16)
        slope = phi + hidden * bell * 0.3989422804014327
        d_active = dot(cotan, w_dn_t[...])
        d_hidden_f = d_active * slope
        d_hidden = d_hidden_f.astype(BF16)
        d_normal = dot(d_hidden, w_up_t[...])
        g = d_normal * gain[...]
        gn = g * normed
        d_cv = inv_std * (
            g - jnp.mean(g, axis=-1, keepdims=True) - normed * jnp.mean(gn, axis=-1, keepdims=True)
        )
        cot_f = cotan.astype(F32)
        g_up[...] += dot(normal_out.T, d_hidden)
        g_dn[...] += dot(cotan.T, active)
        g_bup[...] += jnp.sum(d_hidden_f, axis=0, keepdims=True)
        g_small[0:1] += jnp.sum(d_cv, axis=0, keepdims=True)
        g_small[1:2] += jnp.sum(d_normal * normed, axis=0, keepdims=True)
        g_small[2:3] += jnp.sum(d_normal, axis=0, keepdims=True)
        g_small[3:4] += jnp.sum(cot_f, axis=0, keepdims=True)
        d_low = d_cv.astype(BF16)
        for p in range(2):
            part = d_low[p * half : (p + 1) * half]
            d_turned[p * chans : (p + 1) * chans, pl.ds(pl.multiple_of(first * cols, half), half)] = part.T
            for k in range(count):
                d_conv[2 * (first + k) + p] = part[k * cols : (k + 1) * cols]
        return carry

    lax.fori_loop(0, rows // (2 * count), chunk, 0)

    eye = (
        lax.broadcasted_iota(jnp.int32, (chans, chans), 0)
        == lax.broadcasted_iota(jnp.int32, (chans, chans), 1)
    ).astype(F32)
    pairs = rows // 2

    def tap(b, carry):
        lines = [None] * (taps + 1)
        for q in range(conv_w.shape[0]):
            lanes = pl.ds(pl.multiple_of(b * (2 * chans), 2 * chans), 2 * chans)
            cells = shifted[q : q + pairs, :, lanes].reshape(pairs * cols, 2 * chans)
            both = dot(d_turned[...], cells)
            for p in range(2):
                for s in range(2):
                    a = 2 * q + s - p
                    if 0 <= a < taps:
                        block = both[p * chans : (p + 1) * chans, s * chans : (s + 1) * chans]
                        line = jnp.sum(block * eye, axis=0, keepdims=True)
                        lines[a] = line if lines[a] is None else lines[a] + line
        lines[taps] = jnp.zeros((1, chans), F32)
        g_kern[b] = jnp.concatenate(lines, 0)
        return carry

    lax.fori_loop(0, taps, tap, 0)


def spread_kernel(taps, count, padded, cot, conv_w, out, wide, shifted):
    rows, cols, chans = cot.shape
    spread_taps(padded, wide, shifted, taps)

    def chunk(i, carry):
        first = i * count
        pair_out = conv_pairs(shifted, conv_w, first, count)
        for p in range(2):
            for k in range(count):
                row = 2 * (first + k) + p
                part = pair_out[k * cols : (k + 1) * cols, p * chans : (p + 1) * chans]
                out[row] = (cot[row].astype(F32) + part).astype(BF16)
        return carry

    lax.fori_loop(0, rows // (2 * count), chunk, 0)


def local(
    features,
    cotangent,
    kernel,
    kernel_bias,
    norm_gain,
    norm_shift,
    w_up,
    b_up,
    w_down,
    b_down,
    layer_scale,
):
    taps = kernel.shape[0]
    reach = taps // 2
    rows, cols, chans = features.shape
    units = w_up.shape[1]
    padded_x = widened(features, reach)
    pairs = padded_x.shape[0] // 2
    shapes = jax.ShapeDtypeStruct
    scratch = [
        pltpu.VMEM((2, padded_x.shape[1], chans), F32),
        pltpu.VMEM((pairs, cols, taps * 2 * chans), BF16),
    ]
    vmem = pl.BlockSpec(memory_space=pltpu.VMEM)
    params = pltpu.CompilerParams(vmem_limit_bytes=VMEM_BYTES)
    count = 4
    scaled_down = (w_down.T.astype(F32) * layer_scale[:, None]).astype(BF16)
    with jax.named_scope("forward_back"):
        d_conv, g_up, g_dn, g_bup, g_small, g_kern = pl.pallas_call(
            functools.partial(forward_back, taps, count),
            out_shape=[
                shapes((rows, cols, chans), BF16),
                shapes((chans, units), F32),
                shapes((chans, units), F32),
                shapes((1, units), F32),
                shapes((8, chans), F32),
                shapes((taps, taps + 1, chans), F32),
            ],
            in_specs=[vmem] * 10,
            out_specs=[vmem] * 6,
            scratch_shapes=scratch + [pltpu.VMEM((2 * chans, rows * cols // 2), BF16)],
            compiler_params=params,
        )(
            padded_x,
            cotangent,
            tap_weights(kernel),
            kernel_bias[None],
            norm_gain[None],
            norm_shift[None],
            w_up,
            w_up.T,
            b_up[None],
            scaled_down,
        )
    padded_d = widened(d_conv, reach)
    sums = lax.psum((g_up, g_dn, g_bup, g_small, g_kern), ("gx", "gy"))
    with jax.named_scope("spread"):
        d_features = pl.pallas_call(
            functools.partial(spread_kernel, taps, count),
            out_shape=shapes((rows, cols, chans), BF16),
            in_specs=[vmem] * 3,
            out_specs=vmem,
            scratch_shapes=scratch,
            compiler_params=params,
        )(padded_d, cotangent, tap_weights(kernel[::-1, ::-1]))
    factor = 1.0 / math.sqrt(rows * cols * lax.axis_size("gx") * lax.axis_size("gy"))
    g_up, g_dn, g_bup, g_small, g_kern = [entry * factor for entry in sums]
    d_wdown = g_dn.T * layer_scale
    cot_sum = g_small[3]
    d_lscale = jnp.sum(g_dn.T * w_down.astype(F32), axis=0) + b_down * cot_sum
    return (
        d_features,
        jnp.swapaxes(g_kern[:, :taps], 0, 1),
        g_small[0],
        g_small[1],
        g_small[2],
        g_up,
        g_bup[0],
        d_wdown,
        layer_scale * cot_sum,
        d_lscale,
    )


def solution(mesh):
    placed = (P("gx", "gy", None), P("gx", "gy", None), P(), P(), P(), P(), P(), P(), P(), P(), P())
    return jax.shard_map(
        local,
        mesh=mesh,
        in_specs=placed,
        out_specs=(P("gx", "gy", None), P(), P(), P(), P(), P(), P(), P(), P(), P()),
        check_vma=False,
    )
```

```python
import functools
import math

import jax
import jax.numpy as jnp
from jax import lax
from jax.experimental import pallas as pl
from jax.experimental.pallas import tpu as pltpu
from jax.sharding import PartitionSpec as P

EPSILON = 1e-06
F32 = jnp.float32
BF16 = jnp.bfloat16
VMEM_BYTES = 60 * 1024 * 1024


def dot(left, right):
    return jnp.dot(left, right, preferred_element_type=F32)


def extended(cells, sides, width):
    for axis, dim in sides:
        count = lax.axis_size(axis)
        head = lax.slice_in_dim(cells, 0, width, axis=dim)
        tail = lax.slice_in_dim(cells, cells.shape[dim] - width, cells.shape[dim], axis=dim)
        cells = jnp.concatenate(
            [
                lax.ppermute(tail, axis, [(i, (i + 1) % count) for i in range(count)]),
                cells,
                lax.ppermute(head, axis, [((i + 1) % count, i) for i in range(count)]),
            ],
            axis=dim,
        )
    return cells


def mask_edges(padded, width):
    col_total = padded.shape[1]
    inner_cols = col_total - 2 * width
    grid_cols = inner_cols * lax.axis_size("gy")
    col_place = lax.axis_index("gy") * inner_cols + lax.iota(jnp.int32, col_total) - width
    keep_mask = (col_place >= 0) & (col_place < grid_cols)
    return jnp.where(keep_mask[None, :, None], padded, jnp.zeros((), padded.dtype))


def widened(cells, reach):
    padded = mask_edges(extended(cells, (("gx", 0), ("gy", 1)), reach), reach)
    extra = -padded.shape[1] % 16
    return jnp.pad(padded, ((0, 0), (0, extra), (0, 0)))


def tap_weights(kernel):
    taps, _, chans = kernel.shape
    pairs = (taps + 1) // 2
    framed = jnp.pad(kernel, ((1, 1), (0, 0), (0, 0)))
    eye = jnp.eye(chans, dtype=F32)
    blocks = []
    for q in range(pairs):
        top = jnp.concatenate([framed[2 * q + 1, :, :, None] * eye, framed[2 * q, :, :, None] * eye], 2)
        low = jnp.concatenate([framed[2 * q + 2, :, :, None] * eye, framed[2 * q + 1, :, :, None] * eye], 2)
        blocks.append(jnp.concatenate([top, low], 1).reshape(taps * 2 * chans, 2 * chans))
    return jnp.stack(blocks).astype(BF16)


def spread_taps(padded, wide, shifted, taps):
    pairs, cols, _ = shifted.shape
    chans = padded.shape[2]

    def one(j, carry):
        for s in range(2):
            wide[s] = padded[2 * j + s].astype(F32)
            for b in range(taps):
                at = (2 * b + s) * chans
                shifted[j, :, at : at + chans] = wide[s, b : b + cols, :].astype(BF16)
        return carry

    lax.fori_loop(0, pairs, one, 0)


def conv_pairs(shifted, weights, first, count):
    pairs, cols, depth = shifted.shape
    total = None
    for q in range(weights.shape[0]):
        rows = shifted[pl.ds(first + q, count)].reshape(count * cols, depth)
        part = dot(rows, weights[q])
        total = part if total is None else total + part
    return total


def forward_back(
    taps,
    count,
    padded,
    cot,
    conv_w,
    kbias,
    gain,
    shift,
    w_up,
    w_up_t,
    b_up,
    w_dn_t,
    d_conv,
    packed,
    wide,
    shifted,
    d_turned,
    g_up,
    g_dn,
    g_bup,
    g_small,
):
    rows, cols, chans = cot.shape
    half = count * cols
    spread_taps(padded, wide, shifted, taps)
    g_up[...] = jnp.zeros_like(g_up)
    g_dn[...] = jnp.zeros_like(g_dn)
    g_bup[...] = jnp.zeros_like(g_bup)
    g_small[...] = jnp.zeros_like(g_small)

    def chunk(i, carry):
        first = i * count
        pair_out = conv_pairs(shifted, conv_w, first, count)
        conv = jnp.concatenate([pair_out[:, :chans], pair_out[:, chans:]], 0) + kbias[...]
        cot_rows = [cot[2 * (first + k) + p] for p in range(2) for k in range(count)]
        cotan = jnp.concatenate(cot_rows, 0)
        centred = conv - jnp.mean(conv, axis=-1, keepdims=True)
        inv_std = lax.rsqrt(jnp.mean(centred * centred, axis=-1, keepdims=True) + EPSILON)
        normed = centred * inv_std
        normal_out = (normed * gain[...] + shift[...]).astype(BF16)
        hidden = dot(normal_out, w_up[...]) + b_up[...]
        bell = jnp.exp(hidden * hidden * -0.5)
        place = 1.0 / (1.0 + jnp.abs(hidden) * (0.3275911 * 0.7071067811865476))
        tail = place * (
            0.127414796
            + place * (-0.142248368 + place * (0.7107068705 + place * (-0.7265760135 + place * 0.5307027145)))
        )
        tail = tail * bell
        phi = jnp.where(hidden >= 0.0, 1.0 - tail, tail)
        active = (hidden * phi).astype(BF16)
        slope = phi + hidden * bell * 0.3989422804014327
        d_active = dot(cotan, w_dn_t[...])
        d_hidden_f = d_active * slope
        d_hidden = d_hidden_f.astype(BF16)
        d_normal = dot(d_hidden, w_up_t[...])
        g = d_normal * gain[...]
        gn = g * normed
        d_cv = inv_std * (
            g - jnp.mean(g, axis=-1, keepdims=True) - normed * jnp.mean(gn, axis=-1, keepdims=True)
        )
        cot_f = cotan.astype(F32)
        g_up[...] += dot(normal_out.T, d_hidden)
        g_dn[...] += dot(cotan.T, active)
        g_bup[...] += jnp.sum(d_hidden_f, axis=0, keepdims=True)
        g_small[0:1] += jnp.sum(d_cv, axis=0, keepdims=True)
        g_small[1:2] += jnp.sum(d_normal * normed, axis=0, keepdims=True)
        g_small[2:3] += jnp.sum(d_normal, axis=0, keepdims=True)
        g_small[3:4] += jnp.sum(cot_f, axis=0, keepdims=True)
        d_low = d_cv.astype(BF16)
        for p in range(2):
            part = d_low[p * half : (p + 1) * half]
            d_turned[p * chans : (p + 1) * chans, pl.ds(pl.multiple_of(first * cols, half), half)] = part.T
            for k in range(count):
                d_conv[2 * (first + k) + p] = part[k * cols : (k + 1) * cols]
        return carry

    lax.fori_loop(0, rows // (2 * count), chunk, 0)

    eye = (
        lax.broadcasted_iota(jnp.int32, (chans, chans), 0)
        == lax.broadcasted_iota(jnp.int32, (chans, chans), 1)
    ).astype(F32)
    pairs = rows // 2

    def tap(b, carry):
        lines = [None] * (taps + 1)
        for q in range(conv_w.shape[0]):
            lanes = pl.ds(pl.multiple_of(b * (2 * chans), 2 * chans), 2 * chans)
            cells = shifted[q : q + pairs, :, lanes].reshape(pairs * cols, 2 * chans)
            both = dot(d_turned[...], cells)
            for p in range(2):
                for s in range(2):
                    a = 2 * q + s - p
                    if 0 <= a < taps:
                        block = both[p * chans : (p + 1) * chans, s * chans : (s + 1) * chans]
                        line = jnp.sum(block * eye, axis=0, keepdims=True)
                        lines[a] = line if lines[a] is None else lines[a] + line
        lines[taps] = jnp.zeros((1, chans), F32)
        at = pl.multiple_of(b * (taps + 1), taps + 1)
        packed[pl.ds(at, taps + 1)] = jnp.concatenate(lines, 0)
        return carry

    lax.fori_loop(0, taps, tap, 0)
    at = taps * (taps + 1)
    blocks = g_up.shape[1] // chans
    for kept in (g_up, g_dn):
        for k in range(blocks):
            packed[at : at + chans] = kept[:, k * chans : (k + 1) * chans]
            at += chans
    packed[at : at + 8] = g_small[...]
    at += 8
    packed[at : at + 8] = jnp.concatenate(
        [g_bup[:, k * chans : (k + 1) * chans] for k in range(blocks)]
        + [jnp.zeros((8 - blocks, chans), F32)],
        0,
    )
    at += 8
    packed[at:] = jnp.zeros((packed.shape[0] - at, chans), F32)


def spread_kernel(
    taps, count, nx, ny, padded, cot, conv_w, packed, out, total,
    wide, shifted, got_y, part_y, got_x, whole, s1, r1, s2, r2, s3, r3, s4, r4,
):
    rows, cols, chans = cot.shape
    here_x, here_y = lax.axis_index("gx"), lax.axis_index("gy")
    part = packed.shape[0] // (nx * ny)
    block = part * nx
    others_x = [lax.rem(here_x + d, nx) for d in range(1, nx)]
    others_y = [lax.rem(here_y + d, ny) for d in range(1, ny)]

    def span(index, size):
        return pl.ds(pl.multiple_of(index * size, 8), size)

    def send(src, dst, sent, came, there):
        return pltpu.make_async_remote_copy(
            src_ref=src, dst_ref=dst, send_sem=sent, recv_sem=came,
            device_id=there, device_id_type=pl.DeviceIdType.MESH,
        )

    barrier = pltpu.get_barrier_semaphore()
    for x in others_x:
        pl.semaphore_signal(
            barrier, inc=1, device_id=(x, here_y), device_id_type=pl.DeviceIdType.MESH
        )
    for y in others_y:
        pl.semaphore_signal(
            barrier, inc=1, device_id=(here_x, y), device_id_type=pl.DeviceIdType.MESH
        )
    pl.semaphore_wait(barrier, nx + ny - 2)

    scatter_y = [
        send(packed.at[span(y, block)], got_y.at[d], s1.at[d], r1.at[d], (here_x, y))
        for d, y in enumerate(others_y)
    ]
    for copy in scatter_y:
        copy.start()
    spread_taps(padded, wide, shifted, taps)

    def chunk(i, carry):
        first = i * count
        pair_out = conv_pairs(shifted, conv_w, first, count)
        for p in range(2):
            for k in range(count):
                row = 2 * (first + k) + p
                part_out = pair_out[k * cols : (k + 1) * cols, p * chans : (p + 1) * chans]
                out[row] = (cot[row].astype(F32) + part_out).astype(BF16)
        return carry

    chunks = rows // (2 * count)
    lax.fori_loop(0, chunks // 4, chunk, 0)

    for copy in scatter_y:
        copy.wait()
    mine = packed[span(here_y, block), :]
    for d in range(ny - 1):
        mine = mine + got_y[d]
    part_y[...] = mine
    scatter_x = [
        send(part_y.at[span(x, part)], got_x.at[d], s2.at[d], r2.at[d], (x, here_y))
        for d, x in enumerate(others_x)
    ]
    for copy in scatter_x:
        copy.start()
    lax.fori_loop(chunks // 4, chunks // 2, chunk, 0)

    for copy in scatter_x:
        copy.wait()
    mine = part_y[span(here_x, part), :]
    for d in range(nx - 1):
        mine = mine + got_x[d]
    own = span(here_y * nx + here_x, part)
    whole[own, :] = mine
    gather_x = [
        send(whole.at[own], whole.at[own], s3.at[d], r3.at[d], (x, here_y))
        for d, x in enumerate(others_x)
    ]
    for copy in gather_x:
        copy.start()
    lax.fori_loop(chunks // 2, 3 * chunks // 4, chunk, 0)

    for copy in gather_x:
        copy.wait()
    own = span(here_y, block)
    gather_y = [
        send(whole.at[own], whole.at[own], s4.at[d], r4.at[d], (here_x, y))
        for d, y in enumerate(others_y)
    ]
    for copy in gather_y:
        copy.start()
    lax.fori_loop(3 * chunks // 4, chunks, chunk, 0)
    for copy in gather_y:
        copy.wait()
    total[...] = whole[...]


def local(
    features,
    cotangent,
    kernel,
    kernel_bias,
    norm_gain,
    norm_shift,
    w_up,
    b_up,
    w_down,
    b_down,
    layer_scale,
):
    taps = kernel.shape[0]
    reach = taps // 2
    rows, cols, chans = features.shape
    units = w_up.shape[1]
    padded_x = widened(features, reach)
    pairs = padded_x.shape[0] // 2
    shapes = jax.ShapeDtypeStruct
    scratch = [
        pltpu.VMEM((2, padded_x.shape[1], chans), F32),
        pltpu.VMEM((pairs, cols, taps * 2 * chans), BF16),
    ]
    vmem = pl.BlockSpec(memory_space=pltpu.VMEM)
    params = pltpu.CompilerParams(vmem_limit_bytes=VMEM_BYTES)
    count = 4
    scaled_down = (w_down.T.astype(F32) * layer_scale[:, None]).astype(BF16)
    nx, ny = lax.axis_size("gx"), lax.axis_size("gy")
    blocks = units // chans
    used = taps * (taps + 1) + 2 * blocks * chans + 16
    part = -(-used // (nx * ny * 8)) * 8
    with jax.named_scope("forward_back"):
        d_conv, packed = pl.pallas_call(
            functools.partial(forward_back, taps, count),
            out_shape=[
                shapes((rows, cols, chans), BF16),
                shapes((part * nx * ny, chans), F32),
            ],
            in_specs=[vmem] * 10,
            out_specs=[vmem] * 2,
            scratch_shapes=scratch
            + [
                pltpu.VMEM((2 * chans, rows * cols // 2), BF16),
                pltpu.VMEM((chans, units), F32),
                pltpu.VMEM((chans, units), F32),
                pltpu.VMEM((1, units), F32),
                pltpu.VMEM((8, chans), F32),
            ],
            compiler_params=params,
        )(
            padded_x,
            cotangent,
            tap_weights(kernel),
            kernel_bias[None],
            norm_gain[None],
            norm_shift[None],
            w_up,
            w_up.T,
            b_up[None],
            scaled_down,
        )
    padded_d = widened(d_conv, reach)
    sems = pltpu.SemaphoreType.DMA
    with jax.named_scope("spread"):
        d_features, summed = pl.pallas_call(
            functools.partial(spread_kernel, taps, count, nx, ny),
            out_shape=[
                shapes((rows, cols, chans), BF16),
                shapes((part * nx * ny, chans), F32),
            ],
            in_specs=[vmem] * 4,
            out_specs=[vmem] * 2,
            scratch_shapes=scratch
            + [
                pltpu.VMEM((ny - 1, part * nx, chans), F32),
                pltpu.VMEM((part * nx, chans), F32),
                pltpu.VMEM((nx - 1, part, chans), F32),
                pltpu.VMEM((part * nx * ny, chans), F32),
            ]
            + [sems((ny - 1,))] * 2
            + [sems((nx - 1,))] * 4
            + [sems((ny - 1,))] * 2,
            compiler_params=pltpu.CompilerParams(
                vmem_limit_bytes=VMEM_BYTES, collective_id=0, has_side_effects=True
            ),
        )(padded_d, cotangent, tap_weights(kernel[::-1, ::-1]), packed)
    factor = 1.0 / math.sqrt(rows * cols * nx * ny)
    summed = summed * factor
    at = taps * (taps + 1)
    g_kern = summed[:at].reshape(taps, taps + 1, chans)
    spans = blocks * chans
    g_up = jnp.swapaxes(summed[at : at + spans].reshape(blocks, chans, chans), 0, 1)
    at += spans
    g_dn_t = jnp.swapaxes(summed[at : at + spans].reshape(blocks, chans, chans), 1, 2)
    g_dn_t = g_dn_t.reshape(units, chans)
    at += spans
    g_small = summed[at : at + 8]
    g_bup = summed[at + 8 : at + 8 + blocks].reshape(units)
    cot_sum = g_small[3]
    d_lscale = jnp.sum(g_dn_t * w_down.astype(F32), axis=0) + b_down * cot_sum
    return (
        d_features,
        jnp.swapaxes(g_kern[:, :taps], 0, 1),
        g_small[0],
        g_small[1],
        g_small[2],
        g_up.reshape(chans, units),
        g_bup,
        g_dn_t * layer_scale,
        layer_scale * cot_sum,
        d_lscale,
    )


def solution(mesh):
    placed = (P("gx", "gy", None), P("gx", "gy", None), P(), P(), P(), P(), P(), P(), P(), P(), P())
    return jax.shard_map(
        local,
        mesh=mesh,
        in_specs=placed,
        out_specs=(P("gx", "gy", None), P(), P(), P(), P(), P(), P(), P(), P(), P()),
        check_vma=False,
    )
```

```python
import functools
import math

import jax
import jax.numpy as jnp
from jax import lax
from jax.experimental import pallas as pl
from jax.experimental.pallas import tpu as pltpu
from jax.sharding import PartitionSpec as P

EPSILON = 1e-06
F32 = jnp.float32
BF16 = jnp.bfloat16
VMEM_BYTES = 60 * 1024 * 1024


def dot(left, right):
    return jnp.dot(left, right, preferred_element_type=F32)


def build_weights(kernel, weights, flip):
    taps, _, chans = kernel.shape
    keep = lax.broadcasted_iota(jnp.int32, (chans, chans), 0) == lax.broadcasted_iota(
        jnp.int32, (chans, chans), 1
    )
    for q in range(weights.shape[0]):
        for b in range(taps):
            for s in range(2):
                for p in range(2):
                    a = 2 * q + s - p
                    at = (2 * b + s) * chans
                    if 0 <= a < taps:
                        u, v = (taps - 1 - a, taps - 1 - b) if flip else (a, b)
                        block = jnp.where(keep, kernel[u, v : v + 1, :], 0.0).astype(BF16)
                    else:
                        block = jnp.zeros((chans, chans), BF16)
                    weights[q, at : at + chans, p * chans : (p + 1) * chans] = block


def send(src, dst, sent, came, there):
    return pltpu.make_async_remote_copy(
        src_ref=src,
        dst_ref=dst,
        send_sem=sent,
        recv_sem=came,
        device_id=there,
        device_id_type=pl.DeviceIdType.MESH,
    )


def greet(peers):
    barrier = pltpu.get_barrier_semaphore()
    for there in peers:
        pl.semaphore_signal(
            barrier, inc=1, device_id=there, device_id_type=pl.DeviceIdType.MESH
        )
    pl.semaphore_wait(barrier, len(peers))


def around(nx, ny):
    here_x, here_y = lax.axis_index("gx"), lax.axis_index("gy")
    up, down = lax.rem(here_x + nx - 1, nx), lax.rem(here_x + 1, nx)
    left, right = lax.rem(here_y + ny - 1, ny), lax.rem(here_y + 1, ny)
    return here_x, here_y, up, down, left, right


def pack_edges(cells, edge_out):
    rows, cols, _ = cells.shape

    def group(g, carry):
        for side in range(2):
            at = 0 if side == 0 else cols - 16
            lines = [cells[4 * g + k, at : at + 16, :].astype(F32) for k in range(4)]
            cut = slice(0, 4) if side == 0 else slice(12, 16)
            edge_out[side, g] = jnp.concatenate([line[cut] for line in lines], 0).astype(BF16)
        return carry

    lax.fori_loop(0, rows // 4, group, 0)


def halo_copies(nx, ny, cells, edge_out, edge_in, row_in, sent, came):
    rows = cells.shape[0]
    groups = rows // 4
    here_x, here_y, up, down, left, right = around(nx, ny)
    plain = [
        send(cells.at[0:4], row_in.at[1], sent.at[0], came.at[0], (up, here_y)),
        send(cells.at[rows - 4 : rows], row_in.at[0], sent.at[1], came.at[1], (down, here_y)),
    ]
    sides = []
    for side, column in ((0, left), (1, right)):
        other = 1 - side
        base = 2 + 3 * side
        sides.append(
            [
                send(
                    edge_out.at[side],
                    edge_in.at[other, 1 : groups + 1],
                    sent.at[base],
                    came.at[base],
                    (here_x, column),
                ),
                send(
                    edge_out.at[side, 0],
                    edge_in.at[other, groups + 1],
                    sent.at[base + 1],
                    came.at[base + 1],
                    (up, column),
                ),
                send(
                    edge_out.at[side, groups - 1],
                    edge_in.at[other, 0],
                    sent.at[base + 2],
                    came.at[base + 2],
                    (down, column),
                ),
            ]
        )
    return plain, sides, here_y > 0, here_y < ny - 1


def halo_start(copies, edge_in):
    plain, sides, has_left, has_right = copies
    for copy in plain:
        copy.start()
    for side, has in ((0, has_left), (1, has_right)):

        @pl.when(has)
        def _():
            for copy in sides[side]:
                copy.start()

        @pl.when(jnp.logical_not(has))
        def _():
            edge_in[side] = jnp.zeros(edge_in.shape[1:], BF16)


def halo_wait(copies):
    plain, sides, has_left, has_right = copies
    for copy in plain:
        copy.wait()
    for side, has, back in ((0, has_left, has_right), (1, has_right, has_left)):

        @pl.when(has)
        def _():
            for copy in sides[side]:
                copy.wait_send()

        @pl.when(back)
        def _():
            for copy in sides[side]:
                copy.wait_recv()


def spread_taps(cells, edge_in, row_in, wide, shifted, taps):
    rows, cols, chans = cells.shape
    groups = rows // 4
    reach = taps // 2

    def line(g, k, row):
        wide[k, 8 : 8 + cols, :] = row.astype(F32)
        wide[k, 4:8, :] = edge_in[0, g].astype(F32)[4 * k : 4 * k + 4]
        wide[k, 8 + cols : 12 + cols, :] = edge_in[1, g].astype(F32)[4 * k : 4 * k + 4]
        j = 2 * g + (k + 1) // 2 - 1
        s = (k + 1) % 2
        for b in range(taps):
            at = (2 * b + s) * chans
            start = 8 - reach + b
            shifted[j, :, at : at + chans] = wide[k, start : start + cols, :].astype(BF16)

    for k in range(1, 4):
        line(0, k, row_in[0, k])

    def one(g, carry):
        for k in range(4):
            line(g, k, cells[4 * (g - 1) + k])
        return carry

    lax.fori_loop(1, groups + 1, one, 0)
    for k in range(3):
        line(groups + 1, k, row_in[1, k])


def conv_pairs(shifted, weights, first, count):
    pairs, cols, depth = shifted.shape
    total = None
    for q in range(weights.shape[0]):
        rows = shifted[pl.ds(first + q, count)].reshape(count * cols, depth)
        part = dot(rows, weights[q, :, :])
        total = part if total is None else total + part
    return total


def forward_back(
    taps,
    count,
    nx,
    ny,
    cells,
    cot,
    kernel,
    kbias,
    gain,
    shift,
    w_up,
    w_up_t,
    b_up,
    w_dn_t,
    d_conv,
    packed,
    wide,
    shifted,
    d_turned,
    g_up,
    g_dn,
    g_bup,
    g_small,
    conv_w,
    edge_out,
    edge_in,
    row_in,
    sent,
    came,
):
    rows, cols, chans = cot.shape
    half = count * cols
    here_x, here_y, up, down, left, right = around(nx, ny)
    pack_edges(cells, edge_out)
    greet(
        [(up, here_y), (down, here_y)]
        + [(x, y) for y in (left, right) for x in (here_x, up, down)]
    )
    copies = halo_copies(nx, ny, cells, edge_out, edge_in, row_in, sent, came)
    halo_start(copies, edge_in)
    build_weights(kernel, conv_w, False)
    halo_wait(copies)
    spread_taps(cells, edge_in, row_in, wide, shifted, taps)
    g_up[...] = jnp.zeros_like(g_up)
    g_dn[...] = jnp.zeros_like(g_dn)
    g_bup[...] = jnp.zeros_like(g_bup)
    g_small[...] = jnp.zeros_like(g_small)

    def chunk(i, carry):
        first = i * count
        pair_out = conv_pairs(shifted, conv_w, first, count)
        conv = jnp.concatenate([pair_out[:, :chans], pair_out[:, chans:]], 0) + kbias[...]
        cot_rows = [cot[2 * (first + k) + p] for p in range(2) for k in range(count)]
        cotan = jnp.concatenate(cot_rows, 0)
        centred = conv - jnp.mean(conv, axis=-1, keepdims=True)
        inv_std = lax.rsqrt(jnp.mean(centred * centred, axis=-1, keepdims=True) + EPSILON)
        normed = centred * inv_std
        normal_out = (normed * gain[...] + shift[...]).astype(BF16)
        hidden = dot(normal_out, w_up[...]) + b_up[...]
        bell = jnp.exp(hidden * hidden * -0.5)
        place = 1.0 / (1.0 + jnp.abs(hidden) * (0.3275911 * 0.7071067811865476))
        tail = place * (
            0.127414796
            + place * (-0.142248368 + place * (0.7107068705 + place * (-0.7265760135 + place * 0.5307027145)))
        )
        tail = tail * bell
        phi = jnp.where(hidden >= 0.0, 1.0 - tail, tail)
        active = (hidden * phi).astype(BF16)
        slope = phi + hidden * bell * 0.3989422804014327
        d_active = dot(cotan, w_dn_t[...])
        d_hidden_f = d_active * slope
        d_hidden = d_hidden_f.astype(BF16)
        d_normal = dot(d_hidden, w_up_t[...])
        g = d_normal * gain[...]
        gn = g * normed
        d_cv = inv_std * (
            g - jnp.mean(g, axis=-1, keepdims=True) - normed * jnp.mean(gn, axis=-1, keepdims=True)
        )
        cot_f = cotan.astype(F32)
        g_up[...] += dot(normal_out.T, d_hidden)
        g_dn[...] += dot(cotan.T, active)
        g_bup[...] += jnp.sum(d_hidden_f, axis=0, keepdims=True)
        g_small[0:1] += jnp.sum(d_cv, axis=0, keepdims=True)
        g_small[1:2] += jnp.sum(d_normal * normed, axis=0, keepdims=True)
        g_small[2:3] += jnp.sum(d_normal, axis=0, keepdims=True)
        g_small[3:4] += jnp.sum(cot_f, axis=0, keepdims=True)
        d_low = d_cv.astype(BF16)
        for p in range(2):
            part = d_low[p * half : (p + 1) * half]
            d_turned[p * chans : (p + 1) * chans, pl.ds(pl.multiple_of(first * cols, half), half)] = part.T
            for k in range(count):
                d_conv[2 * (first + k) + p] = part[k * cols : (k + 1) * cols]
        return carry

    lax.fori_loop(0, rows // (2 * count), chunk, 0)

    eye = (
        lax.broadcasted_iota(jnp.int32, (chans, chans), 0)
        == lax.broadcasted_iota(jnp.int32, (chans, chans), 1)
    ).astype(F32)
    pairs = rows // 2

    def tap(b, carry):
        lines = [None] * (taps + 1)
        for q in range(conv_w.shape[0]):
            lanes = pl.ds(pl.multiple_of(b * (2 * chans), 2 * chans), 2 * chans)
            cells = shifted[q : q + pairs, :, lanes].reshape(pairs * cols, 2 * chans)
            both = dot(d_turned[...], cells)
            for p in range(2):
                for s in range(2):
                    a = 2 * q + s - p
                    if 0 <= a < taps:
                        block = both[p * chans : (p + 1) * chans, s * chans : (s + 1) * chans]
                        line = jnp.sum(block * eye, axis=0, keepdims=True)
                        lines[a] = line if lines[a] is None else lines[a] + line
        lines[taps] = jnp.zeros((1, chans), F32)
        at = pl.multiple_of(b * (taps + 1), taps + 1)
        packed[pl.ds(at, taps + 1)] = jnp.concatenate(lines, 0)
        return carry

    lax.fori_loop(0, taps, tap, 0)
    at = taps * (taps + 1)
    blocks = g_up.shape[1] // chans
    for k in range(blocks):
        packed[at : at + chans] = g_up[:, k * chans : (k + 1) * chans]
        at += chans
    for k in range(blocks):
        packed[at : at + chans] = g_dn[:, k * chans : (k + 1) * chans].T
        at += chans
    packed[at : at + 8] = g_small[...]
    at += 8
    packed[at : at + 8] = jnp.concatenate(
        [g_bup[:, k * chans : (k + 1) * chans] for k in range(blocks)]
        + [jnp.zeros((8 - blocks, chans), F32)],
        0,
    )
    at += 8
    packed[at:] = jnp.zeros((packed.shape[0] - at, chans), F32)


def spread_kernel(
    taps, count, nx, ny, factor,
    cells, cot, kernel, packed, w_down, b_down, scale,
    out, o_kern, o_up, o_dn, o_bup, o_small,
    wide, shifted, got_y, part_y, got_x, whole, conv_w, edge_out, edge_in, row_in,
    sent, came, s1, r1, s2, r2, s3, r3, s4, r4,
):
    rows, cols, chans = cot.shape
    here_x, here_y, up, down, left, right = around(nx, ny)
    part = packed.shape[0] // (nx * ny)
    block = part * nx
    others_x = [lax.rem(here_x + d, nx) for d in range(1, nx)]
    others_y = [lax.rem(here_y + d, ny) for d in range(1, ny)]

    def span(index, size):
        return pl.ds(pl.multiple_of(index * size, 8), size)

    pack_edges(cells, edge_out)
    greet(
        [(x, here_y) for x in others_x]
        + [(here_x, y) for y in others_y]
        + [(x, y) for y in (left, right) for x in (up, down)]
    )
    copies = halo_copies(nx, ny, cells, edge_out, edge_in, row_in, sent, came)
    halo_start(copies, edge_in)
    scatter_y = [
        send(packed.at[span(y, block)], got_y.at[d], s1.at[d], r1.at[d], (here_x, y))
        for d, y in enumerate(others_y)
    ]
    for copy in scatter_y:
        copy.start()
    build_weights(kernel, conv_w, True)
    halo_wait(copies)
    spread_taps(cells, edge_in, row_in, wide, shifted, taps)

    def chunk(i, carry):
        first = i * count
        pair_out = conv_pairs(shifted, conv_w, first, count)
        for p in range(2):
            for k in range(count):
                row = 2 * (first + k) + p
                part_out = pair_out[k * cols : (k + 1) * cols, p * chans : (p + 1) * chans]
                out[row] = (cot[row].astype(F32) + part_out).astype(BF16)
        return carry

    chunks = rows // (2 * count)
    lax.fori_loop(0, chunks // 4, chunk, 0)

    for copy in scatter_y:
        copy.wait()
    mine = packed[span(here_y, block), :]
    for d in range(ny - 1):
        mine = mine + got_y[d]
    part_y[...] = mine
    scatter_x = [
        send(part_y.at[span(x, part)], got_x.at[d], s2.at[d], r2.at[d], (x, here_y))
        for d, x in enumerate(others_x)
    ]
    for copy in scatter_x:
        copy.start()
    lax.fori_loop(chunks // 4, chunks // 2, chunk, 0)

    for copy in scatter_x:
        copy.wait()
    mine = part_y[span(here_x, part), :]
    for d in range(nx - 1):
        mine = mine + got_x[d]
    own = span(here_y * nx + here_x, part)
    whole[own, :] = mine
    gather_x = [
        send(whole.at[own], whole.at[own], s3.at[d], r3.at[d], (x, here_y))
        for d, x in enumerate(others_x)
    ]
    for copy in gather_x:
        copy.start()
    lax.fori_loop(chunks // 2, 3 * chunks // 4, chunk, 0)

    for copy in gather_x:
        copy.wait()
    own = span(here_y, block)
    gather_y = [
        send(whole.at[own], whole.at[own], s4.at[d], r4.at[d], (here_x, y))
        for d, y in enumerate(others_y)
    ]
    for copy in gather_y:
        copy.start()
    lax.fori_loop(3 * chunks // 4, chunks, chunk, 0)
    for copy in gather_y:
        copy.wait()
    at = taps * (taps + 1)
    for b in range(taps):
        lines = whole[b * (taps + 1) : (b + 1) * (taps + 1)] * factor
        for a in range(taps):
            o_kern[a, b : b + 1] = lines[a : a + 1]
    blocks = o_up.shape[1] // chans
    for k in range(blocks):
        o_up[:, k * chans : (k + 1) * chans] = whole[at : at + chans] * factor
        at += chans
    kept = jnp.zeros((1, chans), F32)
    for k in range(blocks):
        grad = whole[at : at + chans] * factor
        down_w = w_down[k * chans : (k + 1) * chans].astype(F32)
        kept = kept + jnp.sum(grad * down_w, axis=0, keepdims=True)
        o_dn[k * chans : (k + 1) * chans] = grad * scale[...]
        at += chans
    small = whole[at : at + 8] * factor
    cot_sum = small[3:4]
    o_small[0:3] = small[0:3]
    o_small[3:4] = cot_sum * scale[...]
    o_small[4:5] = kept + b_down[...] * cot_sum
    o_small[5:8] = jnp.zeros((3, chans), F32)
    at += 8
    for k in range(blocks):
        o_bup[:, k * chans : (k + 1) * chans] = whole[at + k : at + k + 1] * factor


def local(
    features,
    cotangent,
    kernel,
    kernel_bias,
    norm_gain,
    norm_shift,
    w_up,
    b_up,
    w_down,
    b_down,
    layer_scale,
):
    taps = kernel.shape[0]
    reach = taps // 2
    rows, cols, chans = features.shape
    units = w_up.shape[1]
    nx, ny = lax.axis_size("gx"), lax.axis_size("gy")
    pairs = (rows + 2 * reach) // 2
    groups = rows // 4
    shapes = jax.ShapeDtypeStruct
    sems = pltpu.SemaphoreType.DMA
    scratch = [
        pltpu.VMEM((4, cols + 16, chans), F32),
        pltpu.VMEM((pairs, cols, taps * 2 * chans), BF16),
    ]
    halo = [
        pltpu.VMEM(((taps + 1) // 2, taps * 2 * chans, 2 * chans), BF16),
        pltpu.VMEM((2, groups, 16, chans), BF16),
        pltpu.VMEM((2, groups + 2, 16, chans), BF16),
        pltpu.VMEM((2, 4, cols, chans), BF16),
        sems((8,)),
        sems((8,)),
    ]
    vmem = pl.BlockSpec(memory_space=pltpu.VMEM)
    count = 4
    scaled_down = (w_down.T.astype(F32) * layer_scale[:, None]).astype(BF16)
    blocks = units // chans
    used = taps * (taps + 1) + 2 * blocks * chans + 16
    part = -(-used // (nx * ny * 8)) * 8
    with jax.named_scope("forward_back"):
        d_conv, packed = pl.pallas_call(
            functools.partial(forward_back, taps, count, nx, ny),
            out_shape=[
                shapes((rows, cols, chans), BF16),
                shapes((part * nx * ny, chans), F32),
            ],
            in_specs=[vmem] * 10,
            out_specs=[vmem] * 2,
            scratch_shapes=scratch
            + [
                pltpu.VMEM((2 * chans, rows * cols // 2), BF16),
                pltpu.VMEM((chans, units), F32),
                pltpu.VMEM((chans, units), F32),
                pltpu.VMEM((1, units), F32),
                pltpu.VMEM((8, chans), F32),
            ]
            + halo,
            compiler_params=pltpu.CompilerParams(
                vmem_limit_bytes=VMEM_BYTES, collective_id=1, has_side_effects=True
            ),
        )(
            features,
            cotangent,
            kernel,
            kernel_bias[None],
            norm_gain[None],
            norm_shift[None],
            w_up,
            w_up.T,
            b_up[None],
            scaled_down,
        )
    factor = 1.0 / math.sqrt(rows * cols * nx * ny)
    with jax.named_scope("spread"):
        d_features, d_kern, d_wup, d_wdown, d_bup, small = pl.pallas_call(
            functools.partial(spread_kernel, taps, count, nx, ny, factor),
            out_shape=[
                shapes((rows, cols, chans), BF16),
                shapes((taps, taps, chans), F32),
                shapes((chans, units), F32),
                shapes((units, chans), F32),
                shapes((1, units), F32),
                shapes((8, chans), F32),
            ],
            in_specs=[vmem] * 7,
            out_specs=[vmem] * 6,
            scratch_shapes=scratch
            + [
                pltpu.VMEM((ny - 1, part * nx, chans), F32),
                pltpu.VMEM((part * nx, chans), F32),
                pltpu.VMEM((nx - 1, part, chans), F32),
                pltpu.VMEM((part * nx * ny, chans), F32),
            ]
            + halo
            + [sems((ny - 1,))] * 2
            + [sems((nx - 1,))] * 4
            + [sems((ny - 1,))] * 2,
            compiler_params=pltpu.CompilerParams(
                vmem_limit_bytes=VMEM_BYTES, collective_id=0, has_side_effects=True
            ),
        )(d_conv, cotangent, kernel, packed, w_down, b_down[None], layer_scale[None])
    return (
        d_features,
        d_kern,
        small[0],
        small[1],
        small[2],
        d_wup,
        d_bup[0],
        d_wdown,
        small[3],
        small[4],
    )


def solution(mesh):
    placed = (P("gx", "gy", None), P("gx", "gy", None), P(), P(), P(), P(), P(), P(), P(), P(), P())
    return jax.shard_map(
        local,
        mesh=mesh,
        in_specs=placed,
        out_specs=(P("gx", "gy", None), P(), P(), P(), P(), P(), P(), P(), P(), P()),
        check_vma=False,
    )
```

```python
import functools
import math

import jax
import jax.numpy as jnp
from jax import lax
from jax.experimental import pallas as pl
from jax.experimental.pallas import tpu as pltpu
from jax.sharding import PartitionSpec as P

EPSILON = 1e-06
F32 = jnp.float32
BF16 = jnp.bfloat16
VMEM_BYTES = 60 * 1024 * 1024


def dot(left, right):
    return jnp.dot(left, right, preferred_element_type=F32)


def build_weights(kernel, weights, flip):
    taps, _, chans = kernel.shape
    keep = lax.broadcasted_iota(jnp.int32, (chans, chans), 0) == lax.broadcasted_iota(
        jnp.int32, (chans, chans), 1
    )
    for q in range(weights.shape[0]):
        for b in range(taps):
            for s in range(2):
                for p in range(2):
                    a = 2 * q + s - p
                    at = (2 * b + s) * chans
                    if 0 <= a < taps:
                        u, v = (taps - 1 - a, taps - 1 - b) if flip else (a, b)
                        block = jnp.where(keep, kernel[u, v : v + 1, :], 0.0).astype(BF16)
                    else:
                        block = jnp.zeros((chans, chans), BF16)
                    weights[q, at : at + chans, p * chans : (p + 1) * chans] = block


def send(src, dst, sent, came, there):
    return pltpu.make_async_remote_copy(
        src_ref=src,
        dst_ref=dst,
        send_sem=sent,
        recv_sem=came,
        device_id=there,
        device_id_type=pl.DeviceIdType.MESH,
    )


def greet(peers):
    barrier = pltpu.get_barrier_semaphore()
    for there in peers:
        pl.semaphore_signal(
            barrier, inc=1, device_id=there, device_id_type=pl.DeviceIdType.MESH
        )
    pl.semaphore_wait(barrier, len(peers))


def around(nx, ny):
    here_x, here_y = lax.axis_index("gx"), lax.axis_index("gy")
    up, down = lax.rem(here_x + nx - 1, nx), lax.rem(here_x + 1, nx)
    left, right = lax.rem(here_y + ny - 1, ny), lax.rem(here_y + 1, ny)
    return here_x, here_y, up, down, left, right


def pack_edges(cells, edge_out):
    rows, cols, _ = cells.shape

    def group(g, carry):
        for side in range(2):
            at = 0 if side == 0 else cols - 16
            lines = [cells[4 * g + k, at : at + 16, :].astype(F32) for k in range(4)]
            cut = slice(0, 4) if side == 0 else slice(12, 16)
            edge_out[side, g] = jnp.concatenate([line[cut] for line in lines], 0).astype(BF16)
        return carry

    lax.fori_loop(0, rows // 4, group, 0)


def halo_copies(nx, ny, cells, edge_out, edge_in, row_in, sent, came):
    rows = cells.shape[0]
    groups = rows // 4
    here_x, here_y, up, down, left, right = around(nx, ny)
    plain = [
        send(cells.at[0:4], row_in.at[1], sent.at[0], came.at[0], (up, here_y)),
        send(cells.at[rows - 4 : rows], row_in.at[0], sent.at[1], came.at[1], (down, here_y)),
    ]
    sides = []
    for side, column in ((0, left), (1, right)):
        other = 1 - side
        base = 2 + 3 * side
        sides.append(
            [
                send(
                    edge_out.at[side],
                    edge_in.at[other, 1 : groups + 1],
                    sent.at[base],
                    came.at[base],
                    (here_x, column),
                ),
                send(
                    edge_out.at[side, 0],
                    edge_in.at[other, groups + 1],
                    sent.at[base + 1],
                    came.at[base + 1],
                    (up, column),
                ),
                send(
                    edge_out.at[side, groups - 1],
                    edge_in.at[other, 0],
                    sent.at[base + 2],
                    came.at[base + 2],
                    (down, column),
                ),
            ]
        )
    return plain, sides, here_y > 0, here_y < ny - 1


def halo_start(copies, edge_in):
    plain, sides, has_left, has_right = copies
    for copy in plain:
        copy.start()
    for side, has in ((0, has_left), (1, has_right)):

        @pl.when(has)
        def _():
            for copy in sides[side]:
                copy.start()

        @pl.when(jnp.logical_not(has))
        def _():
            edge_in[side] = jnp.zeros(edge_in.shape[1:], BF16)


def halo_wait(copies):
    plain, sides, has_left, has_right = copies
    for copy in plain:
        copy.wait()
    for side, has, back in ((0, has_left, has_right), (1, has_right, has_left)):

        @pl.when(has)
        def _():
            for copy in sides[side]:
                copy.wait_send()

        @pl.when(back)
        def _():
            for copy in sides[side]:
                copy.wait_recv()


def spread_taps(cells, edge_in, row_in, wide, shifted, taps):
    rows, cols, chans = cells.shape
    groups = rows // 4
    reach = taps // 2

    def line(g, k, row):
        wide[k, 8 : 8 + cols, :] = row.astype(F32)
        wide[k, 4:8, :] = edge_in[0, g].astype(F32)[4 * k : 4 * k + 4]
        wide[k, 8 + cols : 12 + cols, :] = edge_in[1, g].astype(F32)[4 * k : 4 * k + 4]
        j = 2 * g + (k + 1) // 2 - 1
        s = (k + 1) % 2
        for b in range(taps):
            at = (2 * b + s) * chans
            start = 8 - reach + b
            shifted[j, :, at : at + chans] = wide[k, start : start + cols, :].astype(BF16)

    for k in range(1, 4):
        line(0, k, row_in[0, k])

    def one(g, carry):
        for k in range(4):
            line(g, k, cells[4 * (g - 1) + k])
        return carry

    lax.fori_loop(1, groups + 1, one, 0)
    for k in range(3):
        line(groups + 1, k, row_in[1, k])


def conv_pairs(shifted, weights, first, count):
    pairs, cols, depth = shifted.shape
    total = None
    for q in range(weights.shape[0]):
        rows = shifted[pl.ds(first + q, count)].reshape(count * cols, depth)
        part = dot(rows, weights[q, :, :])
        total = part if total is None else total + part
    return total


def forward_back(
    taps,
    count,
    nx,
    ny,
    cells,
    cot,
    kernel,
    kbias,
    gain,
    shift,
    w_up,
    w_up_t,
    b_up,
    w_dn_t,
    d_conv,
    packed,
    wide,
    shifted,
    d_turned,
    g_up,
    g_dn,
    g_bup,
    g_small,
    ahead,
    conv_w,
    edge_out,
    edge_in,
    row_in,
    sent,
    came,
):
    rows, cols, chans = cot.shape
    half = count * cols
    here_x, here_y, up, down, left, right = around(nx, ny)
    pack_edges(cells, edge_out)
    greet(
        [(up, here_y), (down, here_y)]
        + [(x, y) for y in (left, right) for x in (here_x, up, down)]
    )
    copies = halo_copies(nx, ny, cells, edge_out, edge_in, row_in, sent, came)
    halo_start(copies, edge_in)
    build_weights(kernel, conv_w, False)
    halo_wait(copies)
    spread_taps(cells, edge_in, row_in, wide, shifted, taps)
    g_up[...] = jnp.zeros_like(g_up)
    g_dn[...] = jnp.zeros_like(g_dn)
    g_bup[...] = jnp.zeros_like(g_bup)
    g_small[...] = jnp.zeros_like(g_small)

    chunks = rows // (2 * count)
    ahead[0] = conv_pairs(shifted, conv_w, 0, count)

    def chunk(i, carry):
        first = i * count
        slot = lax.rem(i, 2)
        pair_out = ahead[slot]
        later = lax.rem(i + 1, chunks)
        ahead[1 - slot] = conv_pairs(shifted, conv_w, later * count, count)
        conv = jnp.concatenate([pair_out[:, :chans], pair_out[:, chans:]], 0) + kbias[...]
        cot_rows = [cot[2 * (first + k) + p] for p in range(2) for k in range(count)]
        cotan = jnp.concatenate(cot_rows, 0)
        centred = conv - jnp.mean(conv, axis=-1, keepdims=True)
        inv_std = lax.rsqrt(jnp.mean(centred * centred, axis=-1, keepdims=True) + EPSILON)
        normed = centred * inv_std
        normal_out = (normed * gain[...] + shift[...]).astype(BF16)
        hidden = dot(normal_out, w_up[...]) + b_up[...]
        bell = jnp.exp2(hidden * hidden * (-0.5 * 1.4426950408889634))
        under = 1.0 + jnp.abs(hidden) * (0.3275911 * 0.7071067811865476)
        rough = pl.reciprocal(under, approx=True)
        place = rough * (2.0 - under * rough)
        tail = place * (
            0.127414796
            + place * (-0.142248368 + place * (0.7107068705 + place * (-0.7265760135 + place * 0.5307027145)))
        )
        tail = tail * bell
        phi = jnp.where(hidden >= 0.0, 1.0 - tail, tail)
        active = (hidden * phi).astype(BF16)
        slope = phi + hidden * bell * 0.3989422804014327
        d_active = dot(cotan, w_dn_t[...])
        d_hidden_f = d_active * slope
        d_hidden = d_hidden_f.astype(BF16)
        d_normal = dot(d_hidden, w_up_t[...])
        g = d_normal * gain[...]
        gn = g * normed
        d_cv = inv_std * (
            g - jnp.mean(g, axis=-1, keepdims=True) - normed * jnp.mean(gn, axis=-1, keepdims=True)
        )
        cot_f = cotan.astype(F32)
        g_up[...] += dot(normal_out.T, d_hidden)
        g_dn[...] += dot(cotan.T, active)
        g_bup[...] += jnp.sum(d_hidden_f, axis=0, keepdims=True)
        g_small[0:1] += jnp.sum(d_cv, axis=0, keepdims=True)
        g_small[1:2] += jnp.sum(d_normal * normed, axis=0, keepdims=True)
        g_small[2:3] += jnp.sum(d_normal, axis=0, keepdims=True)
        g_small[3:4] += jnp.sum(cot_f, axis=0, keepdims=True)
        d_low = d_cv.astype(BF16)
        for p in range(2):
            part = d_low[p * half : (p + 1) * half]
            d_turned[p * chans : (p + 1) * chans, pl.ds(pl.multiple_of(first * cols, half), half)] = part.T
            for k in range(count):
                d_conv[2 * (first + k) + p] = part[k * cols : (k + 1) * cols]
        return carry

    lax.fori_loop(0, chunks, chunk, 0)

    eye = (
        lax.broadcasted_iota(jnp.int32, (chans, chans), 0)
        == lax.broadcasted_iota(jnp.int32, (chans, chans), 1)
    ).astype(F32)
    pairs = rows // 2

    def tap(b, carry):
        lines = [None] * (taps + 1)
        for q in range(conv_w.shape[0]):
            lanes = pl.ds(pl.multiple_of(b * (2 * chans), 2 * chans), 2 * chans)
            cells = shifted[q : q + pairs, :, lanes].reshape(pairs * cols, 2 * chans)
            both = dot(d_turned[...], cells)
            for p in range(2):
                for s in range(2):
                    a = 2 * q + s - p
                    if 0 <= a < taps:
                        block = both[p * chans : (p + 1) * chans, s * chans : (s + 1) * chans]
                        line = jnp.sum(block * eye, axis=0, keepdims=True)
                        lines[a] = line if lines[a] is None else lines[a] + line
        lines[taps] = jnp.zeros((1, chans), F32)
        at = pl.multiple_of(b * (taps + 1), taps + 1)
        packed[pl.ds(at, taps + 1)] = jnp.concatenate(lines, 0)
        return carry

    lax.fori_loop(0, taps, tap, 0)
    at = taps * (taps + 1)
    blocks = g_up.shape[1] // chans
    for k in range(blocks):
        packed[at : at + chans] = g_up[:, k * chans : (k + 1) * chans]
        at += chans
    for k in range(blocks):
        packed[at : at + chans] = g_dn[:, k * chans : (k + 1) * chans].T
        at += chans
    packed[at : at + 8] = g_small[...]
    at += 8
    packed[at : at + 8] = jnp.concatenate(
        [g_bup[:, k * chans : (k + 1) * chans] for k in range(blocks)]
        + [jnp.zeros((8 - blocks, chans), F32)],
        0,
    )
    at += 8
    packed[at:] = jnp.zeros((packed.shape[0] - at, chans), F32)


def spread_kernel(
    taps, count, nx, ny, factor,
    cells, cot, kernel, packed, w_down, b_down, scale,
    out, o_kern, o_up, o_dn, o_bup, o_small,
    wide, shifted, got_y, part_y, got_x, whole, conv_w, edge_out, edge_in, row_in,
    sent, came, s1, r1, s2, r2, s3, r3, s4, r4,
):
    rows, cols, chans = cot.shape
    here_x, here_y, up, down, left, right = around(nx, ny)
    part = packed.shape[0] // (nx * ny)
    block = part * nx
    others_x = [lax.rem(here_x + d, nx) for d in range(1, nx)]
    others_y = [lax.rem(here_y + d, ny) for d in range(1, ny)]

    def span(index, size):
        return pl.ds(pl.multiple_of(index * size, 8), size)

    pack_edges(cells, edge_out)
    greet(
        [(x, here_y) for x in others_x]
        + [(here_x, y) for y in others_y]
        + [(x, y) for y in (left, right) for x in (up, down)]
    )
    copies = halo_copies(nx, ny, cells, edge_out, edge_in, row_in, sent, came)
    halo_start(copies, edge_in)
    scatter_y = [
        send(packed.at[span(y, block)], got_y.at[d], s1.at[d], r1.at[d], (here_x, y))
        for d, y in enumerate(others_y)
    ]
    for copy in scatter_y:
        copy.start()
    build_weights(kernel, conv_w, True)
    halo_wait(copies)
    spread_taps(cells, edge_in, row_in, wide, shifted, taps)

    def chunk(i, carry):
        first = i * count
        pair_out = conv_pairs(shifted, conv_w, first, count)
        for p in range(2):
            for k in range(count):
                row = 2 * (first + k) + p
                part_out = pair_out[k * cols : (k + 1) * cols, p * chans : (p + 1) * chans]
                out[row] = (cot[row].astype(F32) + part_out).astype(BF16)
        return carry

    chunks = rows // (2 * count)
    lax.fori_loop(0, chunks // 8, chunk, 0)

    for copy in scatter_y:
        copy.wait()
    mine = packed[span(here_y, block), :]
    for d in range(ny - 1):
        mine = mine + got_y[d]
    part_y[...] = mine
    scatter_x = [
        send(part_y.at[span(x, part)], got_x.at[d], s2.at[d], r2.at[d], (x, here_y))
        for d, x in enumerate(others_x)
    ]
    for copy in scatter_x:
        copy.start()
    lax.fori_loop(chunks // 8, 3 * chunks // 8, chunk, 0)

    for copy in scatter_x:
        copy.wait()
    mine = part_y[span(here_x, part), :]
    for d in range(nx - 1):
        mine = mine + got_x[d]
    own = span(here_y * nx + here_x, part)
    whole[own, :] = mine
    gather_x = [
        send(whole.at[own], whole.at[own], s3.at[d], r3.at[d], (x, here_y))
        for d, x in enumerate(others_x)
    ]
    for copy in gather_x:
        copy.start()
    lax.fori_loop(3 * chunks // 8, 5 * chunks // 8, chunk, 0)

    for copy in gather_x:
        copy.wait()
    own = span(here_y, block)
    gather_y = [
        send(whole.at[own], whole.at[own], s4.at[d], r4.at[d], (here_x, y))
        for d, y in enumerate(others_y)
    ]
    for copy in gather_y:
        copy.start()
    lax.fori_loop(5 * chunks // 8, chunks, chunk, 0)
    for copy in gather_y:
        copy.wait()
    at = taps * (taps + 1)
    for b in range(taps):
        lines = whole[b * (taps + 1) : (b + 1) * (taps + 1)] * factor
        for a in range(taps):
            o_kern[a, b : b + 1] = lines[a : a + 1]
    blocks = o_up.shape[1] // chans
    for k in range(blocks):
        o_up[:, k * chans : (k + 1) * chans] = whole[at : at + chans] * factor
        at += chans
    kept = jnp.zeros((1, chans), F32)
    for k in range(blocks):
        grad = whole[at : at + chans] * factor
        down_w = w_down[k * chans : (k + 1) * chans].astype(F32)
        kept = kept + jnp.sum(grad * down_w, axis=0, keepdims=True)
        o_dn[k * chans : (k + 1) * chans] = grad * scale[...]
        at += chans
    small = whole[at : at + 8] * factor
    cot_sum = small[3:4]
    o_small[0:3] = small[0:3]
    o_small[3:4] = cot_sum * scale[...]
    o_small[4:5] = kept + b_down[...] * cot_sum
    o_small[5:8] = jnp.zeros((3, chans), F32)
    at += 8
    for k in range(blocks):
        o_bup[:, k * chans : (k + 1) * chans] = whole[at + k : at + k + 1] * factor


def local(
    features,
    cotangent,
    kernel,
    kernel_bias,
    norm_gain,
    norm_shift,
    w_up,
    b_up,
    w_down,
    b_down,
    layer_scale,
):
    taps = kernel.shape[0]
    reach = taps // 2
    rows, cols, chans = features.shape
    units = w_up.shape[1]
    nx, ny = lax.axis_size("gx"), lax.axis_size("gy")
    pairs = (rows + 2 * reach) // 2
    groups = rows // 4
    shapes = jax.ShapeDtypeStruct
    sems = pltpu.SemaphoreType.DMA
    scratch = [
        pltpu.VMEM((4, cols + 16, chans), F32),
        pltpu.VMEM((pairs, cols, taps * 2 * chans), BF16),
    ]
    halo = [
        pltpu.VMEM(((taps + 1) // 2, taps * 2 * chans, 2 * chans), BF16),
        pltpu.VMEM((2, groups, 16, chans), BF16),
        pltpu.VMEM((2, groups + 2, 16, chans), BF16),
        pltpu.VMEM((2, 4, cols, chans), BF16),
        sems((8,)),
        sems((8,)),
    ]
    vmem = pl.BlockSpec(memory_space=pltpu.VMEM)
    count = 4
    scaled_down = (w_down.T.astype(F32) * layer_scale[:, None]).astype(BF16)
    blocks = units // chans
    used = taps * (taps + 1) + 2 * blocks * chans + 16
    part = -(-used // (nx * ny * 8)) * 8
    with jax.named_scope("forward_back"):
        d_conv, packed = pl.pallas_call(
            functools.partial(forward_back, taps, count, nx, ny),
            out_shape=[
                shapes((rows, cols, chans), BF16),
                shapes((part * nx * ny, chans), F32),
            ],
            in_specs=[vmem] * 10,
            out_specs=[vmem] * 2,
            scratch_shapes=scratch
            + [
                pltpu.VMEM((2 * chans, rows * cols // 2), BF16),
                pltpu.VMEM((chans, units), F32),
                pltpu.VMEM((chans, units), F32),
                pltpu.VMEM((1, units), F32),
                pltpu.VMEM((8, chans), F32),
                pltpu.VMEM((2, count * cols, 2 * chans), F32),
            ]
            + halo,
            compiler_params=pltpu.CompilerParams(
                vmem_limit_bytes=VMEM_BYTES, collective_id=1, has_side_effects=True
            ),
        )(
            features,
            cotangent,
            kernel,
            kernel_bias[None],
            norm_gain[None],
            norm_shift[None],
            w_up,
            w_up.T,
            b_up[None],
            scaled_down,
        )
    factor = 1.0 / math.sqrt(rows * cols * nx * ny)
    with jax.named_scope("spread"):
        d_features, d_kern, d_wup, d_wdown, d_bup, small = pl.pallas_call(
            functools.partial(spread_kernel, taps, 2 * count, nx, ny, factor),
            out_shape=[
                shapes((rows, cols, chans), BF16),
                shapes((taps, taps, chans), F32),
                shapes((chans, units), F32),
                shapes((units, chans), F32),
                shapes((1, units), F32),
                shapes((8, chans), F32),
            ],
            in_specs=[vmem] * 7,
            out_specs=[vmem] * 6,
            scratch_shapes=scratch
            + [
                pltpu.VMEM((ny - 1, part * nx, chans), F32),
                pltpu.VMEM((part * nx, chans), F32),
                pltpu.VMEM((nx - 1, part, chans), F32),
                pltpu.VMEM((part * nx * ny, chans), F32),
            ]
            + halo
            + [sems((ny - 1,))] * 2
            + [sems((nx - 1,))] * 4
            + [sems((ny - 1,))] * 2,
            compiler_params=pltpu.CompilerParams(
                vmem_limit_bytes=VMEM_BYTES, collective_id=0, has_side_effects=True
            ),
        )(d_conv, cotangent, kernel, packed, w_down, b_down[None], layer_scale[None])
    return (
        d_features,
        d_kern,
        small[0],
        small[1],
        small[2],
        d_wup,
        d_bup[0],
        d_wdown,
        small[3],
        small[4],
    )


def solution(mesh):
    placed = (P("gx", "gy", None), P("gx", "gy", None), P(), P(), P(), P(), P(), P(), P(), P(), P())
    return jax.shard_map(
        local,
        mesh=mesh,
        in_specs=placed,
        out_specs=(P("gx", "gy", None), P(), P(), P(), P(), P(), P(), P(), P(), P()),
        check_vma=False,
    )
```
